256 devices in a mesh: users: 32 (over x, z_hi, core), ctx: 8 (over y, z_lo).
Axes of the slice: x: 4, y: 4, z: 8 (z_hi: 4, z_lo: 2; z = z_hi * 2 + z_lo), core: 2. Of those that a mesh axis runs over, the one named last changes fastest.
Arguments:
- event_embed: bfloat16 [512, 32, 8192], P(('users', 'ctx')), may hold values from -6 to 6
- event_time_bucket: int32 [32, 8192], P('users', 'ctx'), may hold values from 0 to 127
- time_table: float32 [128, 512], replicated, may hold values from -6 to 6
- history_length: int32 [32], P('users'), may hold values from 2048 to 8192, as said below
- w_proj: bfloat16 [512, 2048], replicated, may hold values from -0.25 to 0.25
- w_out: bfloat16 [512, 512], replicated, may hold values from -0.25 to 0.25
Outputs:
- layer_out: bfloat16 [32, 8192, 512], P('users', 'ctx')
The draws below stay inside these ranges and needn't reach their ends.
Inputs may be any that keep to these rules, and one draw needn't show every extreme that they name: `history_length`: one user in every draw has a full history of 8192 events.
All inputs are finite; a program needn't handle non-finite values.
Results may differ from the reference program's by a relative error of at most 0.0068.
Values may be sent and summed in bfloat16 or wider, within the bound.
No kernel may reach another device: no remote copies, remote signals or barrier semaphores. Data moves between devices by JAX's collectives and lax.ppermute only.
A program may use at most 64 MiB of HBM per device.

```python
import jax
import jax.numpy as jnp
from jax import lax

D = 512
H = 8
HEAD_DIM = 64
BUCKETS = 128
BAND = 512
PREFIX = 512
EV_DEV = 1024
USERS = 32
EVENTS = 8192


def draw_history_length(key, part):
    rough = jax.random.randint(key, (USERS,), EVENTS // 4, EVENTS + 1)
    chosen = jax.random.randint(jax.random.fold_in(key, 7), (), 0, USERS)
    return jnp.where(jnp.arange(USERS) == chosen, EVENTS, rough).astype(jnp.int32)


def plant(array, stream_key, low, top_value):
    dims = array.shape
    index_at = [jax.random.randint(jax.random.fold_in(stream_key, axis), (), 0, dims[axis]) for axis in range(len(dims))]
    array = array.at[tuple(index_at)].set(low)
    longest = dims.index(max(dims))
    index_at[longest] = (index_at[longest] + 1) % dims[longest]
    return array.at[tuple(index_at)].set(top_value)


def block_levels(own_key, extent, pieces, smallest, largest):
    def one(axis_at, shards_of):
        draws = jax.random.uniform(jax.random.fold_in(jax.random.fold_in(own_key, 6), axis_at), (shards_of,), jnp.float32, smallest / len(pieces), largest / len(pieces))
        return jnp.repeat(jnp.exp(draws), extent[axis_at] // shards_of).reshape((-1,) + (1,) * (len(extent) - axis_at - 1))

    gain = one(*pieces[0])
    for cut in pieces[1:]:
        gain = gain * one(*cut)
    return gain


def bell_draw(key, extent, scale, reach, split=(), kind=jnp.bfloat16):
    level = block_levels(key, extent, split, -0.22, 0.18) if split else 1.0
    values = jax.random.normal(key, extent, jnp.float32) * scale * level
    return jnp.minimum(jnp.maximum(values, -reach), reach).astype(kind)


def setup_inputs(seed: int = 0) -> dict:
    splits = jax.random.split(jax.random.key(seed), 7)
    return {
        "event_embed": bell_draw(splits[0], (D, USERS, EVENTS), 1.0, 6.0, ((0, 256),)),
        "event_time_bucket": plant(jax.random.randint(splits[1], (USERS, EVENTS), 0, BUCKETS), jax.random.fold_in(splits[1], 1), 0, BUCKETS - 1).astype(jnp.int32),
        "time_table": bell_draw(splits[2], (BUCKETS, D), 1.0, 6.0, (), jnp.float32),
        "history_length": draw_history_length(jax.random.fold_in(splits[6], 71), 0),
        "w_proj": bell_draw(splits[4], (D, 4 * D), D ** -0.5, 0.25),
        "w_out": bell_draw(splits[5], (D, D), D ** -0.5, 0.25),
    }


def one_user(embed_cols, bucket_row, length_one, time_table, w_proj, w_out):
    events = embed_cols.T.astype(jnp.float32) + time_table[bucket_row]
    mean_square = lax.optimization_barrier(lax.optimization_barrier(jnp.mean(events * events, axis=1, keepdims=True)))
    normed = (events * lax.rsqrt(mean_square + 1e-05)).astype(jnp.bfloat16)
    projected = jax.nn.silu(jnp.dot(normed, w_proj, preferred_element_type=jnp.float32)).astype(jnp.bfloat16)
    gating = projected[:, :D]
    value_rows = projected[:, D:2 * D]
    query_rows = projected[:, 2 * D:3 * D]
    key_row_matrix = projected[:, 3 * D:]
    pad_keys = jnp.concatenate([jnp.zeros((BAND, D), jnp.bfloat16), key_row_matrix], axis=0)
    pad_values = jnp.concatenate([jnp.zeros((BAND, D), jnp.bfloat16), value_rows], axis=0)
    q_block = min(512, EV_DEV)
    prefix_keys = key_row_matrix[:PREFIX].astype(jnp.float32).reshape(PREFIX, H, HEAD_DIM)
    prefix_value_rows = value_rows[:PREFIX].astype(jnp.float32).reshape(PREFIX, H, HEAD_DIM)
    prefix_position = jnp.arange(PREFIX, dtype=jnp.int32)
    outputs = []
    for position_shift in range(0, EVENTS, q_block):
        query_pos = position_shift + jnp.arange(q_block, dtype=jnp.int32)
        window_pos = position_shift - BAND + jnp.arange(BAND + q_block, dtype=jnp.int32)
        live_query = query_pos < length_one
        window_ok = (window_pos[None, :] >= 0) & (window_pos[None, :] < length_one) & (window_pos[None, :] <= query_pos[:, None])
        window_ok = window_ok & ((window_pos[None, :] > query_pos[:, None] - BAND) | (window_pos[None, :] < PREFIX)) & live_query[:, None]
        prefix_ok = (prefix_position[None, :] < position_shift - BAND) & (prefix_position[None, :] < length_one) & (prefix_position[None, :] <= query_pos[:, None]) & live_query[:, None]
        key_count = lax.optimization_barrier(jnp.sum(window_ok.astype(jnp.int32), axis=1)) + lax.optimization_barrier(jnp.sum(prefix_ok.astype(jnp.int32), axis=1))
        divisor = jnp.maximum(key_count, 1).astype(jnp.float32)
        query_block = query_rows[position_shift:position_shift + q_block].astype(jnp.float32).reshape(q_block, H, HEAD_DIM)
        window_keys = pad_keys[position_shift:position_shift + BAND + q_block].astype(jnp.float32).reshape(-1, H, HEAD_DIM)
        window_values = pad_values[position_shift:position_shift + BAND + q_block].astype(jnp.float32).reshape(-1, H, HEAD_DIM)
        window_scores = jnp.einsum('qhe,khe->hqk', query_block, window_keys)
        prefix_scores = jnp.einsum('qhe,khe->hqk', query_block, prefix_keys)
        window_weights = (jnp.where(window_ok[None], jax.nn.silu(window_scores), 0.0) / divisor[None, :, None]).astype(jnp.bfloat16)
        prefix_weights = (jnp.where(prefix_ok[None], jax.nn.silu(prefix_scores), 0.0) / divisor[None, :, None]).astype(jnp.bfloat16)
        attended = jnp.einsum('hqk,khe->qhe', window_weights.astype(jnp.float32), window_values)
        attended = attended + jnp.einsum('hqk,khe->qhe', prefix_weights.astype(jnp.float32), prefix_value_rows)
        gated = (attended.reshape(q_block, D) * gating[position_shift:position_shift + q_block].astype(jnp.float32)).astype(jnp.bfloat16)
        outputs.append(jnp.dot(gated, w_out, preferred_element_type=jnp.float32).astype(jnp.bfloat16))
    return jnp.concatenate(outputs, axis=0)

def reference(event_embed, event_time_bucket, time_table, history_length, w_proj, w_out):
    user_ids = jnp.arange(USERS, dtype=jnp.int32)

    def per_user(user_id):
        embed_cols = lax.dynamic_index_in_dim(event_embed, user_id, 1, keepdims=False)
        bucket_row = lax.dynamic_index_in_dim(event_time_bucket, user_id, 0, keepdims=False)
        length_one = lax.dynamic_index_in_dim(history_length, user_id, 0, keepdims=False)
        return one_user(embed_cols, bucket_row, length_one, time_table, w_proj, w_out)
    return lax.map(per_user, user_ids)
```

```python
import jax
import jax.numpy as jnp
from jax import lax
from jax.experimental import pallas as pl
from jax.experimental.pallas import tpu as pltpu
from jax.sharding import PartitionSpec as P

H = 8
HEAD = 64
BAND = 512
PREFIX = 512
D = 512
L = 1024
PAIR = 128
PAIRS = D // PAIR
TILE = 256
BLK = 128
VMEM_LIMIT = 56 * 1024 * 1024
F32 = jnp.float32
BF16 = jnp.bfloat16


def silu_of_half(h):
    return h * jnp.tanh(h) + h


def dot(a, b, dims):
    return lax.dot_general(a, b, (dims, ((), ())), preferred_element_type=F32)


def pack_kernel(x_ref, out_ref, rows, prefix_rows):
    users = x_ref.shape[1]
    blocks = x_ref.shape[2] // BLK
    ctx = out_ref.shape[0] // users
    for k in range(2):
        for u in range(0, users, 16):
            for t in range(blocks):
                part = x_ref[k, u : u + 16, t * BLK : (t + 1) * BLK].astype(F32)
                rows[pl.ds((k * users + u) * blocks + t, 16, stride=blocks), :] = part
                if t < 4:
                    prefix_rows[pl.ds(u * 8 + k * 4 + t, 16, stride=8), :] = part

    def user(u, _):
        head = prefix_rows[pl.ds(pl.multiple_of(u * 8, 8), 8), :]
        for c in range(ctx):
            first = rows[pl.ds(pl.multiple_of(u * blocks + c * 8, 8), 8), :]
            second = rows[pl.ds(pl.multiple_of((users + u) * blocks + c * 8, 8), 8), :]
            out_ref[u * ctx + c] = jnp.concatenate([first, second, head], axis=0).astype(BF16)
        return 0

    lax.fori_loop(0, users, user, 0, unroll=2)


def pack(x, ctx):
    users, events = x.shape[1], x.shape[2]
    return pl.pallas_call(
        pack_kernel,
        out_shape=jax.ShapeDtypeStruct((users * ctx, 24, BLK), BF16),
        in_specs=[pl.BlockSpec(memory_space=pltpu.VMEM)],
        out_specs=pl.BlockSpec(memory_space=pltpu.VMEM),
        scratch_shapes=[
            pltpu.VMEM((2 * users * events // BLK, BLK), F32),
            pltpu.VMEM((users * 8, BLK), F32),
        ],
        compiler_params=pltpu.CompilerParams(vmem_limit_bytes=VMEM_LIMIT),
        name="pack",
    )(x)


def norm_kernel(r_ref, bucket_ref, head_bucket_ref, table_ref, low_ref, high_ref, head_ref, own, pre):
    sources = r_ref.shape[0]
    step = 32

    def widen(i, _):
        s = pl.multiple_of(i * step, step)
        part = r_ref[pl.ds(s, step)].astype(F32)
        own[pl.ds(pl.multiple_of(s * 16, 16 * step), 16 * step), :] = part[:, :16].reshape(16 * step, BLK)
        pre[pl.ds(pl.multiple_of(s * 8, 8 * step), 8 * step), :] = part[:, 16:].reshape(8 * step, BLK)
        return 0

    lax.fori_loop(0, sources // step, widen, 0)
    table = table_ref[...]
    t_hi = table.astype(BF16)
    rest = table - t_hi.astype(F32)
    t_mid = rest.astype(BF16)
    t_low = (rest - t_mid.astype(F32)).astype(BF16)
    parts = jnp.concatenate([t_hi, t_mid, t_low], axis=0)
    slot = lax.broadcasted_iota(jnp.int32, (table.shape[0], BLK), 0)

    def block(columns, buckets, out_ref, row):
        hot = (slot == buckets).astype(BF16)
        hot = jnp.concatenate([hot, hot, hot], axis=0)
        events = columns.T + dot(hot, parts, ((0,), (0,)))
        mean = jnp.sum(events * events, axis=1, keepdims=True) * (1.0 / D)
        out_ref[pl.ds(row, BLK), :] = (events * lax.rsqrt(mean + 1e-05)).astype(BF16)

    for j in (4, 5, 6, 7, 0, 1, 2, 3):
        block(
            own[pl.ds(j, D, stride=8), :],
            bucket_ref[:, j * BLK : (j + 1) * BLK],
            low_ref if j < 4 else high_ref,
            (j % 4) * BLK,
        )
    for j in range(4):
        block(pre[pl.ds(j, D, stride=4), :], head_bucket_ref[:, j * BLK : (j + 1) * BLK], head_ref, j * BLK)


def norm(r, bucket, head_bucket, table):
    half = jax.ShapeDtypeStruct((512, D), BF16)
    return pl.pallas_call(
        norm_kernel,
        out_shape=[half, half, half],
        in_specs=[pl.BlockSpec(memory_space=pltpu.VMEM)] * 4,
        out_specs=[pl.BlockSpec(memory_space=pltpu.VMEM)] * 3,
        scratch_shapes=[pltpu.VMEM((L * D // BLK, BLK), F32), pltpu.VMEM((PREFIX * D // BLK, BLK), F32)],
        compiler_params=pltpu.CompilerParams(vmem_limit_bytes=VMEM_LIMIT),
        name="norm",
    )(r, bucket, head_bucket, table)


def half_silu_proj(rows, weights):
    return silu_of_half(dot(rows, weights, ((1,), (0,))) * 0.5)


def head_masks():
    lane = lax.broadcasted_iota(jnp.int32, (TILE, PAIR), 1)
    return lane < HEAD


def finish(att, gating, scale, w_out):
    gated = (att * scale * gating.astype(F32)).astype(BF16)
    return dot(gated, w_out, ((1,), (0,))).astype(BF16)


def row_scale(first, length):
    pos = first + lax.broadcasted_iota(jnp.int32, (TILE, 1), 0)
    count = jnp.minimum(pos + 1, BAND + PREFIX).astype(F32)
    return jnp.where(pos < length, 1.0 / count, 0.0)


def main_kernel(
    place_ref, low_ref, high_ref, head_ref, w_ref, w_out_ref,
    out_ref, acc_ref, query_ref, gate_ref,
    keys, values, queries, gates, att,
):
    c = place_ref[0]
    length = place_ref[1]
    start = c * L

    for t in range(6):
        src = (head_ref, head_ref, low_ref, low_ref, high_ref, high_ref)[t]
        rows = src[(t % 2) * TILE : (t % 2 + 1) * TILE, :]
        at = slice(t * TILE, (t + 1) * TILE)
        v = half_silu_proj(rows, w_ref[:, D : 2 * D]).astype(BF16)
        k = half_silu_proj(rows, w_ref[:, 3 * D :]).astype(BF16)
        for p in range(PAIRS):
            values[p, at, :] = v[:, p * PAIR : (p + 1) * PAIR]
            keys[p, at, :] = k[:, p * PAIR : (p + 1) * PAIR]
        if t >= 2:
            own = slice((t - 2) * TILE, (t - 1) * TILE)
            q = (half_silu_proj(rows, w_ref[:, 2 * D : 3 * D]).astype(BF16) * 0.5).astype(BF16)
            for p in range(PAIRS):
                queries[p, own, :] = q[:, p * PAIR : (p + 1) * PAIR]
            g = half_silu_proj(rows, w_ref[:, :D]).astype(BF16)
            if t < 4:
                gate_ref[own, :] = g
            else:
                gates[(t - 4) * TILE : (t - 3) * TILE, :] = g

    first_head = head_masks()
    row = lax.broadcasted_iota(jnp.int32, (2 * TILE, TILE), 0)
    a = jnp.where(row < TILE, row, row - TILE)
    b = lax.broadcasted_iota(jnp.int32, (2 * TILE, TILE), 1)
    causal = b <= a
    lag = b - a

    def pair(p, _):
        for t in range(4):
            q = queries[p, t * TILE : (t + 1) * TILE, :]
            zero = jnp.zeros_like(q)
            qq = jnp.concatenate([jnp.where(first_head, q, zero), jnp.where(first_head, zero, q)], axis=0)
            total = jnp.zeros((2 * TILE, PAIR), F32)
            tiles = [("pre", 0), ("pre", 1)]
            if t >= 2:
                tiles.append(("far", t))
            if t >= 1:
                tiles.append(("mid", t + 1))
            tiles.append(("diag", t + 2))
            for kind, kt in tiles:
                at = slice(kt * TILE, (kt + 1) * TILE)
                s = dot(qq, keys[p, at, :], ((1,), (1,)))
                if kind == "diag":
                    s = jnp.where(causal, s, 0.0)
                elif kind == "far":
                    s = jnp.where(causal, 0.0, s)
                elif kind == "pre":
                    s = jnp.where(lag <= start + (t * TILE - BAND - kt * TILE), s, 0.0)
                w = silu_of_half(s).astype(BF16)
                total = total + dot(w, values[p, at, :], ((1,), (0,)))
            att[p, t * TILE : (t + 1) * TILE, :] = jnp.where(first_head, total[:TILE], total[TILE:])
        return 0

    lax.fori_loop(0, PAIRS, pair, 0)

    for p in range(PAIRS):
        acc_ref[p] = att[p, : 2 * TILE, :]
        query_ref[p] = queries[p, : 2 * TILE, :]
    for t in (2, 3):
        whole = jnp.concatenate([att[p, t * TILE : (t + 1) * TILE, :] for p in range(PAIRS)], axis=1)
        here = slice((t - 2) * TILE, (t - 1) * TILE)
        scale = row_scale(start + t * TILE, length)
        out_ref[here, :] = finish(whole, gates[here, :], scale, w_out_ref[...])


def main_part(place, low, high, head, w, w_out):
    vm = pl.BlockSpec(memory_space=pltpu.VMEM)
    return pl.pallas_call(
        main_kernel,
        grid=(1,),
        out_shape=[
            jax.ShapeDtypeStruct((L, D), BF16),
            jax.ShapeDtypeStruct((PAIRS, 512, PAIR), F32),
            jax.ShapeDtypeStruct((PAIRS, 512, PAIR), BF16),
            jax.ShapeDtypeStruct((512, D), BF16),
        ],
        in_specs=[pl.BlockSpec(memory_space=pltpu.SMEM)] + [vm] * 5,
        out_specs=[pl.BlockSpec((512, D), lambda i: (1, 0)), vm, vm, vm],
        scratch_shapes=[
            pltpu.VMEM((PAIRS, PREFIX + L, PAIR), BF16),
            pltpu.VMEM((PAIRS, PREFIX + L, PAIR), BF16),
            pltpu.VMEM((PAIRS, L, PAIR), BF16),
            pltpu.VMEM((512, D), BF16),
            pltpu.VMEM((PAIRS, L, PAIR), F32),
        ],
        compiler_params=pltpu.CompilerParams(vmem_limit_bytes=VMEM_LIMIT),
        cost_estimate=pl.CostEstimate(flops=20_000_000_000, bytes_accessed=8_000_000, transcendentals=0),
        name="main_part",
    )(place, low, high, head, w, w_out)


def edge_kernel(
    place_ref, edge_ref, w_ref, w_out_ref, acc_ref, query_ref, gate_ref, prev_ref,
    out_ref, keys, values,
):
    start = place_ref[0] * L
    length = place_ref[1]
    for t in range(2):
        at = slice(t * TILE, (t + 1) * TILE)
        rows = edge_ref[at, :]
        v = half_silu_proj(rows, w_ref[:, D : 2 * D]).astype(BF16)
        k = half_silu_proj(rows, w_ref[:, 3 * D :]).astype(BF16)
        for p in range(PAIRS):
            values[p, at, :] = v[:, p * PAIR : (p + 1) * PAIR]
            keys[p, at, :] = k[:, p * PAIR : (p + 1) * PAIR]
    first_head = head_masks()
    row = lax.broadcasted_iota(jnp.int32, (2 * TILE, TILE), 0)
    a = jnp.where(row < TILE, row, row - TILE)
    later = lax.broadcasted_iota(jnp.int32, (2 * TILE, TILE), 1) > a
    for t in range(2):
        here = slice(t * TILE, (t + 1) * TILE)
        columns = []
        for p in range(PAIRS):
            q = query_ref[p, here, :]
            zero = jnp.zeros_like(q)
            qq = jnp.concatenate([jnp.where(first_head, q, zero), jnp.where(first_head, zero, q)], axis=0)
            total = jnp.zeros((2 * TILE, PAIR), F32)
            for kt in range(t, 2):
                at = slice(kt * TILE, (kt + 1) * TILE)
                s = dot(qq, keys[p, at, :], ((1,), (1,)))
                if kt == t:
                    s = jnp.where(later, s, 0.0)
                w = silu_of_half(s).astype(BF16)
                total = total + dot(w, values[p, at, :], ((1,), (0,)))
            columns.append(acc_ref[p, here, :] + jnp.where(first_head, total[:TILE], total[TILE:]))
        whole = jnp.concatenate(columns, axis=1)
        out_ref[here, :] = finish(
            whole, gate_ref[here, :], row_scale(start + t * TILE, length), w_out_ref[...]
        )


def edge_part(place, edge, w, w_out, acc, query, gate, prev):
    vm = pl.BlockSpec(memory_space=pltpu.VMEM)
    return pl.pallas_call(
        edge_kernel,
        grid=(1,),
        out_shape=jax.ShapeDtypeStruct((L, D), BF16),
        in_specs=[pl.BlockSpec(memory_space=pltpu.SMEM)] + [vm] * 6 + [pl.BlockSpec(memory_space=pl.ANY)],
        out_specs=pl.BlockSpec((512, D), lambda i: (0, 0)),
        input_output_aliases={7: 0},
        scratch_shapes=[
            pltpu.VMEM((PAIRS, BAND, PAIR), BF16),
            pltpu.VMEM((PAIRS, BAND, PAIR), BF16),
        ],
        compiler_params=pltpu.CompilerParams(vmem_limit_bytes=VMEM_LIMIT),
        name="edge_part",
    )(place, edge, w, w_out, acc, query, gate, prev)


def local(event_embed, event_time_bucket, time_table, history_length, w_proj, w_out):
    ctx = lax.axis_size("ctx")
    c = lax.axis_index("ctx")
    place = jnp.stack([c.astype(jnp.int32), history_length[0]])
    head_bucket = lax.all_gather(event_time_bucket[:, :PREFIX], "ctx", axis=0)[0]
    sent = pack(event_embed, ctx)
    got = lax.all_to_all(sent, ("users", "ctx"), split_axis=0, concat_axis=0, tiled=True)
    low, high, head = norm(got, event_time_bucket, head_bucket, time_table)
    edge = lax.ppermute(high, "ctx", [(i, i + 1) for i in range(ctx - 1)])
    out, acc, query, gate = main_part(place, low, high, head, w_proj, w_out)
    out = edge_part(place, edge, w_proj, w_out, acc, query, gate, out)
    return out[None]


def solution(mesh):
    return jax.shard_map(
        local,
        mesh=mesh,
        in_specs=(P(("users", "ctx"), None, None), P("users", "ctx"), P(), P("users"), P(), P()),
        out_specs=P("users", "ctx", None),
        check_vma=False,
    )
```

```python
import jax
import jax.numpy as jnp
from jax import lax
from jax.experimental import pallas as pl
from jax.experimental.pallas import tpu as pltpu
from jax.sharding import PartitionSpec as P

H = 8
HEAD = 64
BAND = 512
PREFIX = 512
D = 512
L = 1024
PAIR = 128
PAIRS = D // PAIR
TILE = 256
BLK = 128
VMEM_LIMIT = 32 * 1024 * 1024
F32 = jnp.float32
BF16 = jnp.bfloat16
VM = pl.BlockSpec(memory_space=pltpu.VMEM)


def silu_of_half(h):
    return h * jnp.tanh(h) + h


def dot(a, b, dims):
    return lax.dot_general(a, b, (dims, ((), ())), preferred_element_type=F32)


def pack_kernel(x_ref, out_ref, rows, head_rows):
    users = x_ref.shape[1]
    blocks = x_ref.shape[2] // BLK
    ctx = out_ref.shape[0] // users
    for k in range(2):
        for t in range(blocks):
            part = x_ref[k, :, t * BLK : (t + 1) * BLK].astype(F32)
            rows[pl.ds(k * users * blocks + t, users, stride=blocks), :] = part
            if t < 4:
                head_rows[pl.ds(k * 4 + t, users, stride=8), :] = part

    def user(u, _):
        head = head_rows[pl.ds(pl.multiple_of(u * 8, 8), 8), :]
        for c in range(ctx):
            first = rows[pl.ds(pl.multiple_of(u * blocks + c * 8, 8), 8), :]
            second = rows[pl.ds(pl.multiple_of((users + u) * blocks + c * 8, 8), 8), :]
            out_ref[u * ctx + c] = jnp.concatenate([first, second, head], axis=0).astype(BF16)
        return 0

    lax.fori_loop(0, users, user, 0, unroll=2)


def pack(x, ctx):
    users, events = x.shape[1], x.shape[2]
    part = 16
    return pl.pallas_call(
        pack_kernel,
        grid=(users // part,),
        out_shape=jax.ShapeDtypeStruct((users * ctx, 24, BLK), BF16),
        in_specs=[pl.BlockSpec((2, part, events), lambda i: (0, i, 0))],
        out_specs=pl.BlockSpec((part * ctx, 24, BLK), lambda i: (i, 0, 0)),
        scratch_shapes=[
            pltpu.VMEM((2 * part * events // BLK, BLK), F32),
            pltpu.VMEM((part * 8, BLK), F32),
        ],
        compiler_params=pltpu.CompilerParams(vmem_limit_bytes=VMEM_LIMIT),
        name="pack",
    )(x)


def time_parts(table):
    t_hi = table.astype(BF16)
    rest = table - t_hi.astype(F32)
    t_mid = rest.astype(BF16)
    t_low = (rest - t_mid.astype(F32)).astype(BF16)
    return jnp.concatenate([t_hi, t_mid, t_low], axis=0)


def normed(columns, hot, parts):
    hot = hot.astype(BF16)
    hot = jnp.concatenate([hot, hot, hot], axis=0)
    events = columns.T + dot(hot, parts, ((0,), (0,)))
    mean = jnp.sum(events * events, axis=1, keepdims=True) * (1.0 / D)
    return (events * lax.rsqrt(mean + 1e-05)).astype(BF16)


def norm_kernel(r_ref, bucket_ref, table_ref, low_ref, high_ref, pre_ref, own, raw, sem):
    sources = r_ref.shape[0]
    step = sources // 4
    copies = [
        pltpu.make_async_copy(r_ref.at[pl.ds(i * step, step)], raw.at[pl.ds(i * step, step)], sem.at[i])
        for i in range(4)
    ]
    for copy in copies:
        copy.start()
    parts = time_parts(table_ref[...])
    slot = lax.broadcasted_iota(jnp.int32, (table_ref.shape[0], BLK), 0)
    for i, copy in enumerate(copies):
        copy.wait()

        def widen(n, _):
            s = pl.multiple_of(i * step + n * 16, 16)
            part = raw[pl.ds(s, 16)].astype(F32)
            own[pl.ds(pl.multiple_of(s * 16, 256), 256), :] = part[:, :16].reshape(256, BLK)
            pre_ref[pl.ds(pl.multiple_of(s * 8, 128), 128), :] = part[:, 16:].reshape(128, BLK)
            return 0

        lax.fori_loop(0, step // 16, widen, 0)
    for j in (4, 5, 6, 7, 0, 1, 2, 3):
        hot = slot == bucket_ref[:, j * BLK : (j + 1) * BLK]
        out_ref = low_ref if j < 4 else high_ref
        out_ref[(j % 4) * BLK : (j % 4 + 1) * BLK, :] = normed(own[pl.ds(j, D, stride=8), :], hot, parts)


def norm(r, bucket, table):
    half = jax.ShapeDtypeStruct((512, D), BF16)
    return pl.pallas_call(
        norm_kernel,
        out_shape=[half, half, jax.ShapeDtypeStruct((PREFIX * D // BLK, BLK), F32)],
        in_specs=[pl.BlockSpec(memory_space=pl.ANY), VM, VM],
        out_specs=[VM] * 3,
        scratch_shapes=[
            pltpu.VMEM((L * D // BLK, BLK), F32),
            pltpu.VMEM(r.shape, BF16),
            pltpu.SemaphoreType.DMA((4,)),
        ],
        compiler_params=pltpu.CompilerParams(vmem_limit_bytes=VMEM_LIMIT),
        cost_estimate=pl.CostEstimate(flops=1_000_000_000, bytes_accessed=4_000_000, transcendentals=0),
        name="norm",
    )(r, bucket, table)


def store_pairs(ref, at, value):
    value = value.astype(BF16)
    for p in range(PAIRS):
        ref[p, at, :] = value[:, p * PAIR : (p + 1) * PAIR]


def half_silu_proj(rows, weights):
    return silu_of_half(dot(rows, weights, ((1,), (0,))) * 0.5)


def head_masks():
    lane = lax.broadcasted_iota(jnp.int32, (TILE, PAIR), 1)
    return lane < HEAD


def finish(att, gating, scale, w_out):
    gated = (att * scale * gating.astype(F32)).astype(BF16)
    return dot(gated, w_out, ((1,), (0,))).astype(BF16)


def row_scale(first, length):
    pos = first + lax.broadcasted_iota(jnp.int32, (TILE, 1), 0)
    count = jnp.minimum(pos + 1, BAND + PREFIX).astype(F32)
    return jnp.where(pos < length, 1.0 / count, 0.0)


def main_kernel(
    place_ref, low_ref, high_ref, pre_ref, table_ref, w_ref, w_out_ref, *refs,
):
    bucket_refs, refs = refs[: len(refs) - 11], refs[len(refs) - 11 :]
    out_ref, acc_ref, query_ref, gate_ref, keys, values, pre_keys, pre_values, queries, gates, att = refs
    c = place_ref[0]
    length = place_ref[1]
    start = c * L
    parts = time_parts(table_ref[...])
    slot = lax.broadcasted_iota(jnp.int32, (table_ref.shape[0], BLK), 0)
    buckets = bucket_refs[0][...]
    for ref in bucket_refs[1:]:
        buckets = buckets + ref[...]
    for t in range(2):
        rows = jnp.concatenate(
            [
                normed(pre_ref[pl.ds(j, D, stride=4), :], slot == buckets[:, j * BLK : (j + 1) * BLK], parts)
                for j in (2 * t, 2 * t + 1)
            ],
            axis=0,
        )
        at = slice(t * TILE, (t + 1) * TILE)
        store_pairs(pre_values, at, half_silu_proj(rows, w_ref[:, D : 2 * D]))
        store_pairs(pre_keys, at, half_silu_proj(rows, w_ref[:, 3 * D :]))

    for t in range(4):
        here = slice((t % 2) * TILE, (t % 2 + 1) * TILE)
        at = slice(t * TILE, (t + 1) * TILE)
        rows = (low_ref if t < 2 else high_ref)[here, :]
        store_pairs(values, at, half_silu_proj(rows, w_ref[:, D : 2 * D]))
        store_pairs(keys, at, half_silu_proj(rows, w_ref[:, 3 * D :]))
        store_pairs(queries, at, half_silu_proj(rows, w_ref[:, 2 * D : 3 * D]) * 0.5)
        (gate_ref if t < 2 else gates)[here, :] = half_silu_proj(rows, w_ref[:, :D]).astype(BF16)

    first_head = head_masks()
    row = lax.broadcasted_iota(jnp.int32, (2 * TILE, TILE), 0)
    a = jnp.where(row < TILE, row, row - TILE)
    b = lax.broadcasted_iota(jnp.int32, (2 * TILE, TILE), 1)
    causal = b <= a
    lag = b - a

    def pair(p, _):
        for t in range(4):
            q = queries[p, t * TILE : (t + 1) * TILE, :]
            zero = jnp.zeros_like(q)
            qq = jnp.concatenate([jnp.where(first_head, q, zero), jnp.where(first_head, zero, q)], axis=0)
            total = jnp.zeros((2 * TILE, PAIR), F32)
            tiles = [("pre", 0), ("pre", 1)]
            if t >= 2:
                tiles.append(("far", t - 2))
            if t >= 1:
                tiles.append(("mid", t - 1))
            tiles.append(("diag", t))
            for kind, kt in tiles:
                at = slice(kt * TILE, (kt + 1) * TILE)
                k_ref, v_ref = (pre_keys, pre_values) if kind == "pre" else (keys, values)
                s = dot(qq, k_ref[p, at, :], ((1,), (1,)))
                if kind == "diag":
                    s = jnp.where(causal, s, 0.0)
                elif kind == "far":
                    s = jnp.where(causal, 0.0, s)
                elif kind == "pre":
                    s = jnp.where(lag <= start + (t * TILE - BAND - kt * TILE), s, 0.0)
                w = silu_of_half(s).astype(BF16)
                total = total + dot(w, v_ref[p, at, :], ((1,), (0,)))
            att[p, t * TILE : (t + 1) * TILE, :] = jnp.where(first_head, total[:TILE], total[TILE:])
        return 0

    lax.fori_loop(0, PAIRS, pair, 0)

    for p in range(PAIRS):
        acc_ref[p] = att[p, : 2 * TILE, :]
        query_ref[p] = queries[p, : 2 * TILE, :]
    for t in (2, 3):
        whole = jnp.concatenate([att[p, t * TILE : (t + 1) * TILE, :] for p in range(PAIRS)], axis=1)
        here = slice((t - 2) * TILE, (t - 1) * TILE)
        scale = row_scale(start + t * TILE, length)
        out_ref[here, :] = finish(whole, gates[here, :], scale, w_out_ref[...])


def main_part(place, low, high, pre, table, w, w_out, buckets):
    return pl.pallas_call(
        main_kernel,
        grid=(1,),
        out_shape=[
            jax.ShapeDtypeStruct((L, D), BF16),
            jax.ShapeDtypeStruct((PAIRS, 512, PAIR), F32),
            jax.ShapeDtypeStruct((PAIRS, 512, PAIR), BF16),
            jax.ShapeDtypeStruct((512, D), BF16),
        ],
        in_specs=[pl.BlockSpec(memory_space=pltpu.SMEM)] + [VM] * (6 + len(buckets)),
        out_specs=[pl.BlockSpec((512, D), lambda i: (1, 0)), VM, VM, VM],
        scratch_shapes=[
            pltpu.VMEM((PAIRS, L, PAIR), BF16),
            pltpu.VMEM((PAIRS, L, PAIR), BF16),
            pltpu.VMEM((PAIRS, PREFIX, PAIR), BF16),
            pltpu.VMEM((PAIRS, PREFIX, PAIR), BF16),
            pltpu.VMEM((PAIRS, L, PAIR), BF16),
            pltpu.VMEM((512, D), BF16),
            pltpu.VMEM((PAIRS, L, PAIR), F32),
        ],
        compiler_params=pltpu.CompilerParams(vmem_limit_bytes=VMEM_LIMIT),
        cost_estimate=pl.CostEstimate(flops=20_000_000_000, bytes_accessed=8_000_000, transcendentals=0),
        name="main_part",
    )(place, low, high, pre, table, w, w_out, *buckets)


def edge_kernel(
    place_ref, edge_ref, w_ref, w_out_ref, acc_ref, query_ref, gate_ref, prev_ref,
    out_ref, keys, values,
):
    start = place_ref[0] * L
    length = place_ref[1]
    for t in range(2):
        at = slice(t * TILE, (t + 1) * TILE)
        rows = edge_ref[at, :]
        store_pairs(values, at, half_silu_proj(rows, w_ref[:, D : 2 * D]))
        store_pairs(keys, at, half_silu_proj(rows, w_ref[:, 3 * D :]))
    first_head = head_masks()
    row = lax.broadcasted_iota(jnp.int32, (2 * TILE, TILE), 0)
    a = jnp.where(row < TILE, row, row - TILE)
    later = lax.broadcasted_iota(jnp.int32, (2 * TILE, TILE), 1) > a
    for t in range(2):
        here = slice(t * TILE, (t + 1) * TILE)
        columns = []
        for p in range(PAIRS):
            q = query_ref[p, here, :]
            zero = jnp.zeros_like(q)
            qq = jnp.concatenate([jnp.where(first_head, q, zero), jnp.where(first_head, zero, q)], axis=0)
            total = jnp.zeros((2 * TILE, PAIR), F32)
            for kt in range(t, 2):
                at = slice(kt * TILE, (kt + 1) * TILE)
                s = dot(qq, keys[p, at, :], ((1,), (1,)))
                if kt == t:
                    s = jnp.where(later, s, 0.0)
                w = silu_of_half(s).astype(BF16)
                total = total + dot(w, values[p, at, :], ((1,), (0,)))
            columns.append(acc_ref[p, here, :] + jnp.where(first_head, total[:TILE], total[TILE:]))
        whole = jnp.concatenate(columns, axis=1)
        out_ref[here, :] = finish(
            whole, gate_ref[here, :], row_scale(start + t * TILE, length), w_out_ref[...]
        )


def edge_part(place, edge, w, w_out, acc, query, gate, prev):
    return pl.pallas_call(
        edge_kernel,
        grid=(1,),
        out_shape=jax.ShapeDtypeStruct((L, D), BF16),
        in_specs=[pl.BlockSpec(memory_space=pltpu.SMEM)] + [VM] * 6 + [pl.BlockSpec(memory_space=pl.ANY)],
        out_specs=pl.BlockSpec((512, D), lambda i: (0, 0)),
        input_output_aliases={7: 0},
        scratch_shapes=[
            pltpu.VMEM((PAIRS, BAND, PAIR), BF16),
            pltpu.VMEM((PAIRS, BAND, PAIR), BF16),
        ],
        compiler_params=pltpu.CompilerParams(vmem_limit_bytes=VMEM_LIMIT),
        name="edge_part",
    )(place, edge, w, w_out, acc, query, gate, prev)


def local(event_embed, event_time_bucket, time_table, history_length, w_proj, w_out):
    ctx = lax.axis_size("ctx")
    c = lax.axis_index("ctx").astype(jnp.int32)
    place = jnp.stack([c, history_length[0]])
    first = event_time_bucket[:, :PREFIX]
    buckets = [jnp.where(c == 0, first, 0)] + [lax.ppermute(first, "ctx", [(0, k)]) for k in range(1, ctx)]
    got = lax.all_to_all(pack(event_embed, ctx), ("users", "ctx"), split_axis=0, concat_axis=0, tiled=True)
    low, high, pre = norm(got, event_time_bucket, time_table)
    edge = lax.ppermute(high, "ctx", [(i, i + 1) for i in range(ctx - 1)])
    out, acc, query, gate = main_part(place, low, high, pre, time_table, w_proj, w_out, buckets)
    out = edge_part(place, edge, w_proj, w_out, acc, query, gate, out)
    return out[None]


def solution(mesh):
    return jax.shard_map(
        local,
        mesh=mesh,
        in_specs=(P(("users", "ctx"), None, None), P("users", "ctx"), P(), P("users"), P(), P()),
        out_specs=P("users", "ctx", None),
        check_vma=False,
    )
```

```python
import jax
import jax.numpy as jnp
from jax import lax
from jax.experimental import pallas as pl
from jax.experimental.pallas import tpu as pltpu
from jax.sharding import PartitionSpec as P

H = 8
HEAD = 64
BAND = 512
PREFIX = 512
D = 512
L = 1024
PAIR = 128
PAIRS = D // PAIR
TILE = 256
BLK = 128
VMEM_LIMIT = 32 * 1024 * 1024
PACK_LIMIT = 60 * 1024 * 1024
F32 = jnp.float32
BF16 = jnp.bfloat16
VM = pl.BlockSpec(memory_space=pltpu.VMEM)


def silu_of_half(h):
    return h * jnp.tanh(h) + h


def dot(a, b, dims):
    return lax.dot_general(a, b, (dims, ((), ())), preferred_element_type=F32)


def pack_kernel(x_ref, out_ref, rows, head_rows):
    users = x_ref.shape[1]
    blocks = x_ref.shape[2] // BLK
    ctx = out_ref.shape[0] // users
    for k in range(2):
        for t in range(blocks):
            part = x_ref[k, :, t * BLK : (t + 1) * BLK].astype(F32)
            rows[pl.ds(k * users * blocks + t, users, stride=blocks), :] = part
            if t < 4:
                head_rows[pl.ds(k * 4 + t, users, stride=8), :] = part

    def user(u, _):
        head = head_rows[pl.ds(pl.multiple_of(u * 8, 8), 8), :]
        for c in range(ctx):
            first = rows[pl.ds(pl.multiple_of(u * blocks + c * 8, 8), 8), :]
            second = rows[pl.ds(pl.multiple_of((users + u) * blocks + c * 8, 8), 8), :]
            out_ref[u * ctx + c] = jnp.concatenate([first, second, head], axis=0).astype(BF16)
        return 0

    lax.fori_loop(0, users, user, 0, unroll=2)


def pack(x, ctx):
    users, events = x.shape[1], x.shape[2]
    part = 16
    return pl.pallas_call(
        pack_kernel,
        grid=(users // part,),
        out_shape=jax.ShapeDtypeStruct((users * ctx, 24, BLK), BF16),
        in_specs=[pl.BlockSpec((2, part, events), lambda i: (0, i, 0))],
        out_specs=pl.BlockSpec((part * ctx, 24, BLK), lambda i: (i, 0, 0)),
        scratch_shapes=[
            pltpu.VMEM((2 * part * events // BLK, BLK), F32),
            pltpu.VMEM((part * 8, BLK), F32),
        ],
        compiler_params=pltpu.CompilerParams(vmem_limit_bytes=PACK_LIMIT),
        name="pack",
    )(x)


def time_parts(table):
    t_hi = table.astype(BF16)
    rest = table - t_hi.astype(F32)
    t_mid = rest.astype(BF16)
    t_low = (rest - t_mid.astype(F32)).astype(BF16)
    return jnp.concatenate([t_hi, t_mid, t_low], axis=0)


def normed(columns, hot, parts):
    hot = hot.astype(BF16)
    hot = jnp.concatenate([hot, hot, hot], axis=0)
    events = columns.T + dot(hot, parts, ((0,), (0,)))
    mean = jnp.sum(events * events, axis=1, keepdims=True) * (1.0 / D)
    return (events * lax.rsqrt(mean + 1e-05)).astype(BF16)


def norm_kernel(r_ref, bucket_ref, table_ref, low_ref, high_ref, pre_ref, own, raw, sem):
    sources = r_ref.shape[0]
    step = sources // 4
    copies = [
        pltpu.make_async_copy(r_ref.at[pl.ds(i * step, step)], raw.at[pl.ds(i * step, step)], sem.at[i])
        for i in range(4)
    ]
    for copy in copies:
        copy.start()
    parts = time_parts(table_ref[...])
    slot = lax.broadcasted_iota(jnp.int32, (table_ref.shape[0], BLK), 0)
    for i, copy in enumerate(copies):
        copy.wait()

        def widen(n, _):
            s = pl.multiple_of(i * step + n * 16, 16)
            part = raw[pl.ds(s, 16)].astype(F32)
            own[pl.ds(pl.multiple_of(s * 16, 256), 256), :] = part[:, :16].reshape(256, BLK)
            pre_ref[pl.ds(pl.multiple_of(s * 8, 128), 128), :] = part[:, 16:].reshape(128, BLK)
            return 0

        lax.fori_loop(0, step // 16, widen, 0)
    for j in (4, 5, 6, 7, 0, 1, 2, 3):
        hot = slot == bucket_ref[:, j * BLK : (j + 1) * BLK]
        out_ref = low_ref if j < 4 else high_ref
        out_ref[(j % 4) * BLK : (j % 4 + 1) * BLK, :] = normed(own[pl.ds(j, D, stride=8), :], hot, parts)


def norm(r, bucket, table):
    half = jax.ShapeDtypeStruct((512, D), BF16)
    return pl.pallas_call(
        norm_kernel,
        out_shape=[half, half, jax.ShapeDtypeStruct((PREFIX * D // BLK, BLK), F32)],
        in_specs=[pl.BlockSpec(memory_space=pl.ANY), VM, VM],
        out_specs=[VM] * 3,
        scratch_shapes=[
            pltpu.VMEM((L * D // BLK, BLK), F32),
            pltpu.VMEM(r.shape, BF16),
            pltpu.SemaphoreType.DMA((4,)),
        ],
        compiler_params=pltpu.CompilerParams(vmem_limit_bytes=VMEM_LIMIT),
        cost_estimate=pl.CostEstimate(flops=1_000_000_000, bytes_accessed=4_000_000, transcendentals=0),
        name="norm",
    )(r, bucket, table)


def store_turned(ref, at, value):
    turned = value.astype(BF16).T
    for p in range(PAIRS):
        ref[p, :, at] = turned[p * PAIR : (p + 1) * PAIR, :]


def store_pairs(ref, at, value):
    value = value.astype(BF16)
    for p in range(PAIRS):
        ref[p, at, :] = value[:, p * PAIR : (p + 1) * PAIR]


def half_silu_proj(rows, weights):
    return silu_of_half(dot(rows, weights, ((1,), (0,))) * 0.5)


def head_masks():
    lane = lax.broadcasted_iota(jnp.int32, (TILE, PAIR), 1)
    return lane < HEAD


def finish(att, gating, scale, w_out):
    gated = (att * scale * gating.astype(F32)).astype(BF16)
    return dot(gated, w_out, ((1,), (0,))).astype(BF16)


def row_scale(first, length):
    pos = first + lax.broadcasted_iota(jnp.int32, (TILE, 1), 0)
    count = jnp.minimum(pos + 1, BAND + PREFIX).astype(F32)
    return jnp.where(pos < length, 1.0 / count, 0.0)


def main_kernel(
    place_ref, low_ref, high_ref, pre_ref, table_ref, w_ref, w_out_ref, *refs,
):
    bucket_refs, refs = refs[: len(refs) - 11], refs[len(refs) - 11 :]
    out_ref, acc_ref, query_ref, gate_ref, keys, values, pre_keys, pre_values, queries, gates, att = refs
    c = place_ref[0]
    length = place_ref[1]
    start = c * L
    parts = time_parts(table_ref[...])
    slot = lax.broadcasted_iota(jnp.int32, (table_ref.shape[0], BLK), 0)
    buckets = bucket_refs[0][...]
    for ref in bucket_refs[1:]:
        buckets = buckets + ref[...]
    for t in range(2):
        rows = jnp.concatenate(
            [
                normed(pre_ref[pl.ds(j, D, stride=4), :], slot == buckets[:, j * BLK : (j + 1) * BLK], parts)
                for j in (2 * t, 2 * t + 1)
            ],
            axis=0,
        )
        at = slice(t * TILE, (t + 1) * TILE)
        store_pairs(pre_values, at, half_silu_proj(rows, w_ref[:, D : 2 * D]))
        store_turned(pre_keys, at, half_silu_proj(rows, w_ref[:, 3 * D :]))

    for t in range(4):
        here = slice((t % 2) * TILE, (t % 2 + 1) * TILE)
        at = slice(t * TILE, (t + 1) * TILE)
        rows = (low_ref if t < 2 else high_ref)[here, :]
        store_pairs(values, at, half_silu_proj(rows, w_ref[:, D : 2 * D]))
        store_turned(keys, at, half_silu_proj(rows, w_ref[:, 3 * D :]))
        store_pairs(queries, at, half_silu_proj(rows, w_ref[:, 2 * D : 3 * D]) * 0.5)
        (gate_ref if t < 2 else gates)[here, :] = half_silu_proj(rows, w_ref[:, :D]).astype(BF16)

    first_head = head_masks()
    row = lax.broadcasted_iota(jnp.int32, (2 * TILE, TILE), 0)
    a = jnp.where(row < TILE, row, row - TILE)
    b = lax.broadcasted_iota(jnp.int32, (2 * TILE, TILE), 1)
    causal = b <= a
    lag = b - a

    def pair(p, _):
        stack = []
        for t in range(4):
            q = queries[p, t * TILE : (t + 1) * TILE, :]
            zero = jnp.zeros_like(q)
            stack += [jnp.where(first_head, q, zero), jnp.where(first_head, zero, q)]
        totals = [None] * 4
        for kind, kt in (("own", 0), ("own", 1), ("own", 2), ("own", 3), ("pre", 0), ("pre", 1)):
            at = slice(kt * TILE, (kt + 1) * TILE)
            k_ref, v_ref = (pre_keys, pre_values) if kind == "pre" else (keys, values)
            here = range(4) if kind == "pre" else range(kt, min(kt + 3, 4))
            for group in ([here[i : i + 4] for i in range(0, len(here), 4)]):
                qq = jnp.concatenate(stack[2 * group[0] : 2 * group[-1] + 2], axis=0)
                s = dot(qq, k_ref[p, :, at], ((1,), (0,)))
                ws = []
                for n, t in enumerate(group):
                    x = s[n * 2 * TILE : (n + 1) * 2 * TILE]
                    if kind == "pre":
                        x = jnp.where(lag <= start + (t * TILE - BAND - kt * TILE), x, 0.0)
                    elif kt == t:
                        x = jnp.where(causal, x, 0.0)
                    elif kt == t - 2:
                        x = jnp.where(causal, 0.0, x)
                    ws.append(silu_of_half(x).astype(BF16))
                o = dot(jnp.concatenate(ws, axis=0), v_ref[p, at, :], ((1,), (0,)))
                for n, t in enumerate(group):
                    x = o[n * 2 * TILE : (n + 1) * 2 * TILE]
                    totals[t] = x if totals[t] is None else totals[t] + x
        for t in range(4):
            att[p, t * TILE : (t + 1) * TILE, :] = jnp.where(first_head, totals[t][:TILE], totals[t][TILE:])
        return 0

    for p in range(PAIRS):
        pair(p, 0)

    for p in range(PAIRS):
        acc_ref[p] = att[p, : 2 * TILE, :]
        query_ref[p] = queries[p, : 2 * TILE, :]
    for t in (2, 3):
        whole = jnp.concatenate([att[p, t * TILE : (t + 1) * TILE, :] for p in range(PAIRS)], axis=1)
        here = slice((t - 2) * TILE, (t - 1) * TILE)
        scale = row_scale(start + t * TILE, length)
        out_ref[here, :] = finish(whole, gates[here, :], scale, w_out_ref[...])


def main_part(place, low, high, pre, table, w, w_out, buckets):
    return pl.pallas_call(
        main_kernel,
        grid=(1,),
        out_shape=[
            jax.ShapeDtypeStruct((L, D), BF16),
            jax.ShapeDtypeStruct((PAIRS, 512, PAIR), F32),
            jax.ShapeDtypeStruct((PAIRS, 512, PAIR), BF16),
            jax.ShapeDtypeStruct((512, D), BF16),
        ],
        in_specs=[pl.BlockSpec(memory_space=pltpu.SMEM)] + [VM] * (6 + len(buckets)),
        out_specs=[pl.BlockSpec((512, D), lambda i: (1, 0)), VM, VM, VM],
        scratch_shapes=[
            pltpu.VMEM((PAIRS, PAIR, L), BF16),
            pltpu.VMEM((PAIRS, L, PAIR), BF16),
            pltpu.VMEM((PAIRS, PAIR, PREFIX), BF16),
            pltpu.VMEM((PAIRS, PREFIX, PAIR), BF16),
            pltpu.VMEM((PAIRS, L, PAIR), BF16),
            pltpu.VMEM((512, D), BF16),
            pltpu.VMEM((PAIRS, L, PAIR), F32),
        ],
        compiler_params=pltpu.CompilerParams(vmem_limit_bytes=VMEM_LIMIT),
        cost_estimate=pl.CostEstimate(flops=20_000_000_000, bytes_accessed=8_000_000, transcendentals=0),
        name="main_part",
    )(place, low, high, pre, table, w, w_out, *buckets)


def edge_kernel(
    place_ref, edge_ref, w_ref, w_out_ref, acc_ref, query_ref, gate_ref, prev_ref,
    out_ref, keys, values,
):
    start = place_ref[0] * L
    length = place_ref[1]
    for t in range(2):
        at = slice(t * TILE, (t + 1) * TILE)
        rows = edge_ref[at, :]
        store_pairs(values, at, half_silu_proj(rows, w_ref[:, D : 2 * D]))
        store_turned(keys, at, half_silu_proj(rows, w_ref[:, 3 * D :]))
    first_head = head_masks()
    row = lax.broadcasted_iota(jnp.int32, (2 * TILE, TILE), 0)
    a = jnp.where(row < TILE, row, row - TILE)
    later = lax.broadcasted_iota(jnp.int32, (2 * TILE, TILE), 1) > a
    for t in range(2):
        here = slice(t * TILE, (t + 1) * TILE)
        columns = []
        for p in range(PAIRS):
            q = query_ref[p, here, :]
            zero = jnp.zeros_like(q)
            qq = jnp.concatenate([jnp.where(first_head, q, zero), jnp.where(first_head, zero, q)], axis=0)
            total = jnp.zeros((2 * TILE, PAIR), F32)
            for kt in range(t, 2):
                at = slice(kt * TILE, (kt + 1) * TILE)
                s = dot(qq, keys[p, :, at], ((1,), (0,)))
                if kt == t:
                    s = jnp.where(later, s, 0.0)
                w = silu_of_half(s).astype(BF16)
                total = total + dot(w, values[p, at, :], ((1,), (0,)))
            columns.append(acc_ref[p, here, :] + jnp.where(first_head, total[:TILE], total[TILE:]))
        whole = jnp.concatenate(columns, axis=1)
        out_ref[here, :] = finish(
            whole, gate_ref[here, :], row_scale(start + t * TILE, length), w_out_ref[...]
        )


def edge_part(place, edge, w, w_out, acc, query, gate, prev):
    return pl.pallas_call(
        edge_kernel,
        grid=(1,),
        out_shape=jax.ShapeDtypeStruct((L, D), BF16),
        in_specs=[pl.BlockSpec(memory_space=pltpu.SMEM)] + [VM] * 6 + [pl.BlockSpec(memory_space=pl.ANY)],
        out_specs=pl.BlockSpec((512, D), lambda i: (0, 0)),
        input_output_aliases={7: 0},
        scratch_shapes=[
            pltpu.VMEM((PAIRS, PAIR, BAND), BF16),
            pltpu.VMEM((PAIRS, BAND, PAIR), BF16),
        ],
        compiler_params=pltpu.CompilerParams(vmem_limit_bytes=VMEM_LIMIT),
        name="edge_part",
    )(place, edge, w, w_out, acc, query, gate, prev)


def local(event_embed, event_time_bucket, time_table, history_length, w_proj, w_out):
    ctx = lax.axis_size("ctx")
    c = lax.axis_index("ctx").astype(jnp.int32)
    place = jnp.stack([c, history_length[0]])
    first = event_time_bucket[:, :PREFIX]
    buckets = [jnp.where(c == 0, first, 0)] + [lax.ppermute(first, "ctx", [(0, k)]) for k in range(1, ctx)]
    got = lax.all_to_all(pack(event_embed, ctx), ("users", "ctx"), split_axis=0, concat_axis=0, tiled=True)
    low, high, pre = norm(got, event_time_bucket, time_table)
    edge = lax.ppermute(high, "ctx", [(i, i + 1) for i in range(ctx - 1)])
    out, acc, query, gate = main_part(place, low, high, pre, time_table, w_proj, w_out, buckets)
    out = edge_part(place, edge, w_proj, w_out, acc, query, gate, out)
    return out[None]


def solution(mesh):
    return jax.shard_map(
        local,
        mesh=mesh,
        in_specs=(P(("users", "ctx"), None, None), P("users", "ctx"), P(), P("users"), P(), P()),
        out_specs=P("users", "ctx", None),
        check_vma=False,
    )
```

```python
import jax
import jax.numpy as jnp
from jax import lax
from jax.experimental import pallas as pl
from jax.experimental.pallas import tpu as pltpu
from jax.sharding import PartitionSpec as P

H = 8
HEAD = 64
BAND = 512
PREFIX = 512
D = 512
L = 1024
PAIR = 128
PAIRS = D // PAIR
TILE = 256
BLK = 128
VMEM_LIMIT = 32 * 1024 * 1024
PACK_LIMIT = 60 * 1024 * 1024
F32 = jnp.float32
BF16 = jnp.bfloat16
VM = pl.BlockSpec(memory_space=pltpu.VMEM)


def silu_of_half(h):
    return h * jnp.tanh(h) + h


def dot(a, b, dims):
    return lax.dot_general(a, b, (dims, ((), ())), preferred_element_type=F32)


def pack_kernel(x_ref, out_ref, rows, head_rows):
    users = x_ref.shape[1]
    blocks = x_ref.shape[2] // BLK
    ctx = out_ref.shape[0] // users
    pitch = rows.shape[0] // (2 * users)
    for k in range(2):
        for t in range(blocks):
            part = x_ref[k, :, t * BLK : (t + 1) * BLK].astype(F32)
            rows[pl.ds(k * users * pitch + t, users, stride=pitch), :] = part
            if t < 4:
                head_rows[pl.ds(k * 4 + t, users, stride=8), :] = part

    def user(u, _):
        head = head_rows[pl.ds(pl.multiple_of(u * 8, 8), 8), :]
        for c in range(ctx):
            first = rows[pl.ds(pl.multiple_of(u * pitch + c * 8, 8), 8), :]
            second = rows[pl.ds(pl.multiple_of((users + u) * pitch + c * 8, 8), 8), :]
            out_ref[u * ctx + c] = jnp.concatenate([first, second, head], axis=0).astype(BF16)
        return 0

    lax.fori_loop(0, users, user, 0, unroll=8)


def pack(x, ctx):
    users, events = x.shape[1], x.shape[2]
    part = 16
    return pl.pallas_call(
        pack_kernel,
        grid=(users // part,),
        out_shape=jax.ShapeDtypeStruct((users * ctx, 24, BLK), BF16),
        in_specs=[pl.BlockSpec((2, part, events), lambda i: (0, i, 0))],
        out_specs=pl.BlockSpec((part * ctx, 24, BLK), lambda i: (i, 0, 0)),
        scratch_shapes=[
            pltpu.VMEM((2 * part * (events // BLK + 8), BLK), F32),
            pltpu.VMEM((part * 8, BLK), F32),
        ],
        compiler_params=pltpu.CompilerParams(vmem_limit_bytes=PACK_LIMIT),
        name="pack",
    )(x)


def time_parts(table):
    t_hi = table.astype(BF16)
    rest = table - t_hi.astype(F32)
    t_mid = rest.astype(BF16)
    t_low = (rest - t_mid.astype(F32)).astype(BF16)
    return jnp.concatenate([t_hi, t_mid, t_low], axis=0)


def normed(columns, hot, parts):
    hot = hot.astype(BF16)
    hot = jnp.concatenate([hot, hot, hot], axis=0)
    events = columns.T + dot(hot, parts, ((0,), (0,)))
    mean = jnp.sum(events * events, axis=1, keepdims=True) * (1.0 / D)
    return (events * lax.rsqrt(mean + 1e-05)).astype(BF16)


def norm_kernel(r_ref, bucket_ref, table_ref, low_ref, high_ref, pre_ref, own, raw, sem):
    sources = r_ref.shape[0]
    step = sources // 4
    copies = [
        pltpu.make_async_copy(r_ref.at[pl.ds(i * step, step)], raw.at[pl.ds(i * step, step)], sem.at[i])
        for i in range(4)
    ]
    for copy in copies:
        copy.start()
    parts = time_parts(table_ref[...])
    slot = lax.broadcasted_iota(jnp.int32, (table_ref.shape[0], BLK), 0)
    for i, copy in enumerate(copies):
        copy.wait()

        def widen(n, _):
            s = pl.multiple_of(i * step + n * 16, 16)
            part = raw[pl.ds(s, 16)].astype(F32)
            own[pl.ds(pl.multiple_of(s * 16, 256), 256), :] = part[:, :16].reshape(256, BLK)
            pre_ref[pl.ds(pl.multiple_of(s * 8, 128), 128), :] = part[:, 16:].reshape(128, BLK)
            return 0

        lax.fori_loop(0, step // 16, widen, 0, unroll=4)
    for j in (4, 5, 6, 7, 0, 1, 2, 3):
        hot = slot == bucket_ref[:, j * BLK : (j + 1) * BLK]
        out_ref = low_ref if j < 4 else high_ref
        out_ref[(j % 4) * BLK : (j % 4 + 1) * BLK, :] = normed(own[pl.ds(j, D, stride=8), :], hot, parts)


def norm(r, bucket, table):
    half = jax.ShapeDtypeStruct((512, D), BF16)
    return pl.pallas_call(
        norm_kernel,
        out_shape=[half, half, jax.ShapeDtypeStruct((PREFIX * D // BLK, BLK), F32)],
        in_specs=[pl.BlockSpec(memory_space=pl.ANY), VM, VM],
        out_specs=[VM] * 3,
        scratch_shapes=[
            pltpu.VMEM((L * D // BLK, BLK), F32),
            pltpu.VMEM(r.shape, BF16),
            pltpu.SemaphoreType.DMA((4,)),
        ],
        compiler_params=pltpu.CompilerParams(vmem_limit_bytes=VMEM_LIMIT),
        cost_estimate=pl.CostEstimate(flops=1_000_000_000, bytes_accessed=4_000_000, transcendentals=0),
        name="norm",
    )(r, bucket, table)


def store_turned(ref, at, value):
    turned = value.astype(BF16).T
    for p in range(PAIRS):
        ref[p, :, at] = turned[p * PAIR : (p + 1) * PAIR, :]


def store_pairs(ref, at, value):
    value = value.astype(BF16)
    for p in range(PAIRS):
        ref[p, at, :] = value[:, p * PAIR : (p + 1) * PAIR]


def half_silu_proj(rows, weights):
    return silu_of_half(dot(rows, weights, ((1,), (0,))) * 0.5)


def head_masks():
    lane = lax.broadcasted_iota(jnp.int32, (TILE, PAIR), 1)
    return lane < HEAD


def finish(att, gating, scale, w_out):
    gated = (att * scale * gating.astype(F32)).astype(BF16)
    return dot(gated, w_out, ((1,), (0,))).astype(BF16)


def row_scale(first, length):
    pos = first + lax.broadcasted_iota(jnp.int32, (TILE, 1), 0)
    count = jnp.minimum(pos + 1, BAND + PREFIX).astype(F32)
    return jnp.where(pos < length, 1.0 / count, 0.0)


def main_kernel(
    place_ref, low_ref, high_ref, pre_ref, table_ref, w_ref, w_out_ref, *refs,
):
    bucket_refs, refs = refs[: len(refs) - 11], refs[len(refs) - 11 :]
    out_ref, acc_ref, query_ref, gate_ref, keys, values, pre_keys, pre_values, queries, gates, att = refs
    c = place_ref[0]
    length = place_ref[1]
    start = c * L
    parts = time_parts(table_ref[...])
    slot = lax.broadcasted_iota(jnp.int32, (table_ref.shape[0], BLK), 0)
    buckets = bucket_refs[0][...]
    for ref in bucket_refs[1:]:
        buckets = buckets + ref[...]
    for t in range(2):
        rows = jnp.concatenate(
            [
                normed(pre_ref[pl.ds(j, D, stride=4), :], slot == buckets[:, j * BLK : (j + 1) * BLK], parts)
                for j in (2 * t, 2 * t + 1)
            ],
            axis=0,
        )
        at = slice(t * TILE, (t + 1) * TILE)
        store_pairs(pre_values, at, half_silu_proj(rows, w_ref[:, D : 2 * D]))
        store_turned(pre_keys, at, half_silu_proj(rows, w_ref[:, 3 * D :]))

    for t in range(4):
        here = slice((t % 2) * TILE, (t % 2 + 1) * TILE)
        at = slice(t * TILE, (t + 1) * TILE)
        rows = (low_ref if t < 2 else high_ref)[here, :]
        store_pairs(values, at, half_silu_proj(rows, w_ref[:, D : 2 * D]))
        store_turned(keys, at, half_silu_proj(rows, w_ref[:, 3 * D :]))
        store_pairs(queries, at, half_silu_proj(rows, w_ref[:, 2 * D : 3 * D]) * 0.5)
        (gate_ref if t < 2 else gates)[here, :] = half_silu_proj(rows, w_ref[:, :D]).astype(BF16)

    first_head = head_masks()
    row = lax.broadcasted_iota(jnp.int32, (2 * TILE, TILE), 0)
    a = jnp.where(row < TILE, row, row - TILE)
    b = lax.broadcasted_iota(jnp.int32, (2 * TILE, TILE), 1)
    causal = b <= a
    lag = b - a

    def pair(p, _):
        stack = []
        for t in range(4):
            q = queries[p, t * TILE : (t + 1) * TILE, :]
            zero = jnp.zeros_like(q)
            stack += [jnp.where(first_head, q, zero), jnp.where(first_head, zero, q)]
        totals = [None] * 4
        for kind, kt in (("own", 0), ("own", 1), ("own", 2), ("own", 3), ("pre", 0), ("pre", 1)):
            at = slice(kt * TILE, (kt + 1) * TILE)
            k_ref, v_ref = (pre_keys, pre_values) if kind == "pre" else (keys, values)
            here = range(4) if kind == "pre" else range(kt, min(kt + 3, 4))
            for group in ([here[i : i + 4] for i in range(0, len(here), 4)]):
                qq = jnp.concatenate(stack[2 * group[0] : 2 * group[-1] + 2], axis=0)
                s = dot(qq, k_ref[p, :, at], ((1,), (0,)))
                ws = []
                for n, t in enumerate(group):
                    x = s[n * 2 * TILE : (n + 1) * 2 * TILE]
                    if kind == "pre":
                        x = jnp.where(lag <= start + (t * TILE - BAND - kt * TILE), x, 0.0)
                    elif kt == t:
                        x = jnp.where(causal, x, 0.0)
                    elif kt == t - 2:
                        x = jnp.where(causal, 0.0, x)
                    ws.append(silu_of_half(x).astype(BF16))
                o = dot(jnp.concatenate(ws, axis=0), v_ref[p, at, :], ((1,), (0,)))
                for n, t in enumerate(group):
                    x = o[n * 2 * TILE : (n + 1) * 2 * TILE]
                    totals[t] = x if totals[t] is None else totals[t] + x
        for t in range(4):
            att[p, t * TILE : (t + 1) * TILE, :] = jnp.where(first_head, totals[t][:TILE], totals[t][TILE:])
        return 0

    for p in range(PAIRS):
        pair(p, 0)

    for p in range(PAIRS):
        acc_ref[p] = att[p, : 2 * TILE, :]
        query_ref[p] = queries[p, : 2 * TILE, :]
    for t in (2, 3):
        whole = jnp.concatenate([att[p, t * TILE : (t + 1) * TILE, :] for p in range(PAIRS)], axis=1)
        here = slice((t - 2) * TILE, (t - 1) * TILE)
        scale = row_scale(start + t * TILE, length)
        out_ref[here, :] = finish(whole, gates[here, :], scale, w_out_ref[...])


def main_part(place, low, high, pre, table, w, w_out, buckets):
    return pl.pallas_call(
        main_kernel,
        grid=(1,),
        out_shape=[
            jax.ShapeDtypeStruct((L, D), BF16),
            jax.ShapeDtypeStruct((PAIRS, 512, PAIR), F32),
            jax.ShapeDtypeStruct((PAIRS, 512, PAIR), BF16),
            jax.ShapeDtypeStruct((512, D), BF16),
        ],
        in_specs=[pl.BlockSpec(memory_space=pltpu.SMEM)] + [VM] * (6 + len(buckets)),
        out_specs=[pl.BlockSpec((512, D), lambda i: (1, 0)), VM, VM, VM],
        scratch_shapes=[
            pltpu.VMEM((PAIRS, PAIR, L), BF16),
            pltpu.VMEM((PAIRS, L, PAIR), BF16),
            pltpu.VMEM((PAIRS, PAIR, PREFIX), BF16),
            pltpu.VMEM((PAIRS, PREFIX, PAIR), BF16),
            pltpu.VMEM((PAIRS, L, PAIR), BF16),
            pltpu.VMEM((512, D), BF16),
            pltpu.VMEM((PAIRS, L, PAIR), F32),
        ],
        compiler_params=pltpu.CompilerParams(vmem_limit_bytes=VMEM_LIMIT),
        cost_estimate=pl.CostEstimate(flops=20_000_000_000, bytes_accessed=8_000_000, transcendentals=0),
        name="main_part",
    )(place, low, high, pre, table, w, w_out, *buckets)


def edge_kernel(
    place_ref, edge_ref, w_ref, w_out_ref, acc_ref, query_ref, gate_ref, prev_ref,
    out_ref, keys, values,
):
    start = place_ref[0] * L
    length = place_ref[1]
    for t in range(2):
        at = slice(t * TILE, (t + 1) * TILE)
        rows = edge_ref[at, :]
        store_pairs(values, at, half_silu_proj(rows, w_ref[:, D : 2 * D]))
        store_turned(keys, at, half_silu_proj(rows, w_ref[:, 3 * D :]))
    first_head = head_masks()
    row = lax.broadcasted_iota(jnp.int32, (2 * TILE, TILE), 0)
    a = jnp.where(row < TILE, row, row - TILE)
    later = lax.broadcasted_iota(jnp.int32, (2 * TILE, TILE), 1) > a
    for t in range(2):
        here = slice(t * TILE, (t + 1) * TILE)
        columns = []
        for p in range(PAIRS):
            q = query_ref[p, here, :]
            zero = jnp.zeros_like(q)
            qq = jnp.concatenate([jnp.where(first_head, q, zero), jnp.where(first_head, zero, q)], axis=0)
            total = jnp.zeros((2 * TILE, PAIR), F32)
            for kt in range(t, 2):
                at = slice(kt * TILE, (kt + 1) * TILE)
                s = dot(qq, keys[p, :, at], ((1,), (0,)))
                if kt == t:
                    s = jnp.where(later, s, 0.0)
                w = silu_of_half(s).astype(BF16)
                total = total + dot(w, values[p, at, :], ((1,), (0,)))
            columns.append(acc_ref[p, here, :] + jnp.where(first_head, total[:TILE], total[TILE:]))
        whole = jnp.concatenate(columns, axis=1)
        out_ref[here, :] = finish(
            whole, gate_ref[here, :], row_scale(start + t * TILE, length), w_out_ref[...]
        )


def edge_part(place, edge, w, w_out, acc, query, gate, prev):
    return pl.pallas_call(
        edge_kernel,
        grid=(1,),
        out_shape=jax.ShapeDtypeStruct((L, D), BF16),
        in_specs=[pl.BlockSpec(memory_space=pltpu.SMEM)] + [VM] * 6 + [pl.BlockSpec(memory_space=pl.ANY)],
        out_specs=pl.BlockSpec((512, D), lambda i: (0, 0)),
        input_output_aliases={7: 0},
        scratch_shapes=[
            pltpu.VMEM((PAIRS, PAIR, BAND), BF16),
            pltpu.VMEM((PAIRS, BAND, PAIR), BF16),
        ],
        compiler_params=pltpu.CompilerParams(vmem_limit_bytes=VMEM_LIMIT),
        name="edge_part",
    )(place, edge, w, w_out, acc, query, gate, prev)


def local(event_embed, event_time_bucket, time_table, history_length, w_proj, w_out):
    ctx = lax.axis_size("ctx")
    c = lax.axis_index("ctx").astype(jnp.int32)
    place = jnp.stack([c, history_length[0]])
    first = event_time_bucket[:, :PREFIX]
    buckets = [jnp.where(c == 0, first, 0)] + [lax.ppermute(first, "ctx", [(0, k)]) for k in range(1, ctx)]
    got = lax.all_to_all(pack(event_embed, ctx), ("users", "ctx"), split_axis=0, concat_axis=0, tiled=True)
    low, high, pre = norm(got, event_time_bucket, time_table)
    edge = lax.ppermute(high, "ctx", [(i, i + 1) for i in range(ctx - 1)])
    out, acc, query, gate = main_part(place, low, high, pre, time_table, w_proj, w_out, buckets)
    out = edge_part(place, edge, w_proj, w_out, acc, query, gate, out)
    return out[None]


def solution(mesh):
    return jax.shard_map(
        local,
        mesh=mesh,
        in_specs=(P(("users", "ctx"), None, None), P("users", "ctx"), P(), P("users"), P(), P()),
        out_specs=P("users", "ctx", None),
        check_vma=False,
    )
```

```python
import jax
import jax.numpy as jnp
from jax import lax
from jax.experimental import pallas as pl
from jax.experimental.pallas import tpu as pltpu
from jax.sharding import PartitionSpec as P

H = 8
HEAD = 64
BAND = 512
PREFIX = 512
D = 512
L = 1024
PAIR = 128
PAIRS = D // PAIR
TILE = 256
BLK = 128
VMEM_LIMIT = 32 * 1024 * 1024
PACK_LIMIT = 60 * 1024 * 1024
F32 = jnp.float32
BF16 = jnp.bfloat16
VM = pl.BlockSpec(memory_space=pltpu.VMEM)


def silu_of_half(h):
    return h * jnp.tanh(h) + h


def dot(a, b, dims):
    return lax.dot_general(a, b, (dims, ((), ())), preferred_element_type=F32)


def pack_kernel(x_ref, out_ref, rows, head_rows):
    users = x_ref.shape[1]
    blocks = x_ref.shape[2] // BLK
    ctx = out_ref.shape[0] // users
    pitch = rows.shape[0] // (2 * users)
    for k in range(2):
        for t in range(blocks):
            part = x_ref[k, :, t * BLK : (t + 1) * BLK].astype(F32)
            rows[pl.ds(k * users * pitch + t, users, stride=pitch), :] = part
            if t < 4:
                head_rows[pl.ds(k * 4 + t, users, stride=8), :] = part

    def user(u, _):
        head = head_rows[pl.ds(pl.multiple_of(u * 8, 8), 8), :]
        for c in range(ctx):
            first = rows[pl.ds(pl.multiple_of(u * pitch + c * 8, 8), 8), :]
            second = rows[pl.ds(pl.multiple_of((users + u) * pitch + c * 8, 8), 8), :]
            out_ref[u * ctx + c] = jnp.concatenate([first, second, head], axis=0).astype(BF16)
        return 0

    lax.fori_loop(0, users, user, 0, unroll=8)


def pack(x, ctx):
    users, events = x.shape[1], x.shape[2]
    part = 16
    return pl.pallas_call(
        pack_kernel,
        grid=(users // part,),
        out_shape=jax.ShapeDtypeStruct((users * ctx, 24, BLK), BF16),
        in_specs=[pl.BlockSpec((2, part, events), lambda i: (0, i, 0))],
        out_specs=pl.BlockSpec((part * ctx, 24, BLK), lambda i: (i, 0, 0)),
        scratch_shapes=[
            pltpu.VMEM((2 * part * (events // BLK + 8), BLK), F32),
            pltpu.VMEM((part * 8, BLK), F32),
        ],
        compiler_params=pltpu.CompilerParams(vmem_limit_bytes=PACK_LIMIT),
        name="pack",
    )(x)


def time_parts(table):
    t_hi = table.astype(BF16)
    rest = table - t_hi.astype(F32)
    t_mid = rest.astype(BF16)
    t_low = (rest - t_mid.astype(F32)).astype(BF16)
    return jnp.concatenate([t_hi, t_mid, t_low], axis=0)


def normed(columns, hot, parts):
    hot = hot.astype(BF16)
    hot = jnp.concatenate([hot, hot, hot], axis=0)
    events = columns.T + dot(hot, parts, ((0,), (0,)))
    mean = jnp.sum(events * events, axis=1, keepdims=True) * (1.0 / D)
    return (events * lax.rsqrt(mean + 1e-05)).astype(BF16)


def norm_kernel(r_ref, bucket_ref, table_ref, low_ref, high_ref, pre_ref, own, raw, sem):
    sources = r_ref.shape[0]
    step = sources // 4
    copies = [
        pltpu.make_async_copy(r_ref.at[pl.ds(i * step, step)], raw.at[pl.ds(i * step, step)], sem.at[i])
        for i in range(4)
    ]
    for copy in copies:
        copy.start()
    parts = time_parts(table_ref[...])
    slot = lax.broadcasted_iota(jnp.int32, (table_ref.shape[0], BLK), 0)
    for i, copy in enumerate(copies):
        copy.wait()

        def widen(n, _):
            s = pl.multiple_of(i * step + n * 16, 16)
            part = raw[pl.ds(s, 16)].astype(F32)
            own[pl.ds(pl.multiple_of(s * 16, 256), 256), :] = part[:, :16].reshape(256, BLK)
            pre_ref[pl.ds(pl.multiple_of(s * 8, 128), 128), :] = part[:, 16:].reshape(128, BLK)
            return 0

        lax.fori_loop(0, step // 16, widen, 0, unroll=4)
    for j in (4, 5, 6, 7, 0, 1, 2, 3):
        hot = slot == bucket_ref[:, j * BLK : (j + 1) * BLK]
        out_ref = low_ref if j < 4 else high_ref
        out_ref[(j % 4) * BLK : (j % 4 + 1) * BLK, :] = normed(own[pl.ds(j, D, stride=8), :], hot, parts)


def norm(r, bucket, table):
    half = jax.ShapeDtypeStruct((512, D), BF16)
    return pl.pallas_call(
        norm_kernel,
        out_shape=[half, half, jax.ShapeDtypeStruct((PREFIX * D // BLK, BLK), F32)],
        in_specs=[pl.BlockSpec(memory_space=pl.ANY), VM, VM],
        out_specs=[VM] * 3,
        scratch_shapes=[
            pltpu.VMEM((L * D // BLK, BLK), F32),
            pltpu.VMEM(r.shape, BF16),
            pltpu.SemaphoreType.DMA((4,)),
        ],
        compiler_params=pltpu.CompilerParams(vmem_limit_bytes=VMEM_LIMIT),
        cost_estimate=pl.CostEstimate(flops=1_000_000_000, bytes_accessed=4_000_000, transcendentals=0),
        name="norm",
    )(r, bucket, table)


def store_turned(ref, at, value):
    turned = value.astype(BF16).T
    for p in range(PAIRS):
        ref[p, :, at] = turned[p * PAIR : (p + 1) * PAIR, :]


def store_pairs(ref, at, value):
    value = value.astype(BF16)
    for p in range(PAIRS):
        ref[p, at, :] = value[:, p * PAIR : (p + 1) * PAIR]


def half_silu_proj(rows, weights):
    return silu_of_half(dot(rows, weights, ((1,), (0,))) * 0.5)


def head_masks():
    lane = lax.broadcasted_iota(jnp.int32, (TILE, PAIR), 1)
    return lane < HEAD


def finish(att, gating, scale, w_out):
    gated = (att * scale * gating.astype(F32)).astype(BF16)
    return dot(gated, w_out, ((1,), (0,))).astype(BF16)


def row_scale(first, length):
    pos = first + lax.broadcasted_iota(jnp.int32, (TILE, 1), 0)
    count = jnp.minimum(pos + 1, BAND + PREFIX).astype(F32)
    return jnp.where(pos < length, 1.0 / count, 0.0)


def main_kernel(
    place_ref, low_ref, high_ref, pre_ref, table_ref, w_ref, w_out_ref, *refs,
):
    bucket_refs, refs = refs[: len(refs) - 11], refs[len(refs) - 11 :]
    out_ref, acc_ref, query_ref, gate_ref, keys, values, pre_keys, pre_values, queries, gates, att = refs
    c = place_ref[0]
    length = place_ref[1]
    start = c * L
    parts = time_parts(table_ref[...])
    slot = lax.broadcasted_iota(jnp.int32, (table_ref.shape[0], BLK), 0)
    buckets = bucket_refs[0][...]
    for ref in bucket_refs[1:]:
        buckets = buckets + ref[...]
    for t in range(2):
        rows = jnp.concatenate(
            [
                normed(pre_ref[pl.ds(j, D, stride=4), :], slot == buckets[:, j * BLK : (j + 1) * BLK], parts)
                for j in (2 * t, 2 * t + 1)
            ],
            axis=0,
        )
        at = slice(t * TILE, (t + 1) * TILE)
        store_pairs(pre_values, at, half_silu_proj(rows, w_ref[:, D : 2 * D]))
        store_turned(pre_keys, at, half_silu_proj(rows, w_ref[:, 3 * D :]))

    for t in range(4):
        here = slice((t % 2) * TILE, (t % 2 + 1) * TILE)
        at = slice(t * TILE, (t + 1) * TILE)
        rows = (low_ref if t < 2 else high_ref)[here, :]
        store_pairs(values, at, half_silu_proj(rows, w_ref[:, D : 2 * D]))
        store_turned(keys, at, half_silu_proj(rows, w_ref[:, 3 * D :]))
        store_pairs(queries, at, half_silu_proj(rows, w_ref[:, 2 * D : 3 * D]) * 0.5)
        (gate_ref if t < 2 else gates)[here, :] = half_silu_proj(rows, w_ref[:, :D]).astype(BF16)

    first_head = head_masks()
    row = lax.broadcasted_iota(jnp.int32, (2 * TILE, TILE), 0)
    a = jnp.where(row < TILE, row, row - TILE)
    b = lax.broadcasted_iota(jnp.int32, (2 * TILE, TILE), 1)
    causal = b <= a
    lag = b - a

    def pair(p, _):
        stack = []
        for t in range(4):
            q = queries[p, t * TILE : (t + 1) * TILE, :]
            zero = jnp.zeros_like(q)
            stack += [jnp.where(first_head, q, zero), jnp.where(first_head, zero, q)]
        totals = [None] * 4
        for kind, kt in (("own", 0), ("own", 1), ("own", 2), ("own", 3), ("pre", 0), ("pre", 1)):
            at = slice(kt * TILE, (kt + 1) * TILE)
            k_ref, v_ref = (pre_keys, pre_values) if kind == "pre" else (keys, values)
            here = range(4) if kind == "pre" else range(kt, min(kt + 3, 4))
            for group in ([here[i : i + 4] for i in range(0, len(here), 4)]):
                qq = jnp.concatenate(stack[2 * group[0] : 2 * group[-1] + 2], axis=0)
                s = dot(qq, k_ref[p, :, at], ((1,), (0,)))
                ws = []
                for n, t in enumerate(group):
                    x = s[n * 2 * TILE : (n + 1) * 2 * TILE]
                    if kind == "pre":
                        x = jnp.where(lag <= start + (t * TILE - BAND - kt * TILE), x, 0.0)
                    elif kt == t:
                        x = jnp.where(causal, x, 0.0)
                    elif kt == t - 2:
                        x = jnp.where(causal, 0.0, x)
                    ws.append(silu_of_half(x).astype(BF16))
                o = dot(jnp.concatenate(ws, axis=0), v_ref[p, at, :], ((1,), (0,)))
                for n, t in enumerate(group):
                    x = o[n * 2 * TILE : (n + 1) * 2 * TILE]
                    totals[t] = x if totals[t] is None else totals[t] + x
        for t in range(4):
            part = jnp.where(first_head, totals[t][:TILE], totals[t][TILE:])
            if t < 2:
                acc_ref[p, t * TILE : (t + 1) * TILE, :] = part
            else:
                att[p, t * TILE : (t + 1) * TILE, :] = part
        return 0

    for p in range(PAIRS):
        pair(p, 0)

    for p in range(PAIRS):
        query_ref[p] = queries[p, : 2 * TILE, :]
    for t in (2, 3):
        whole = jnp.concatenate([att[p, t * TILE : (t + 1) * TILE, :] for p in range(PAIRS)], axis=1)
        here = slice((t - 2) * TILE, (t - 1) * TILE)
        scale = row_scale(start + t * TILE, length)
        out_ref[here, :] = finish(whole, gates[here, :], scale, w_out_ref[...])


def main_part(place, low, high, pre, table, w, w_out, buckets):
    return pl.pallas_call(
        main_kernel,
        grid=(1,),
        out_shape=[
            jax.ShapeDtypeStruct((L, D), BF16),
            jax.ShapeDtypeStruct((PAIRS, 512, PAIR), F32),
            jax.ShapeDtypeStruct((PAIRS, 512, PAIR), BF16),
            jax.ShapeDtypeStruct((512, D), BF16),
        ],
        in_specs=[pl.BlockSpec(memory_space=pltpu.SMEM)] + [VM] * (6 + len(buckets)),
        out_specs=[pl.BlockSpec((512, D), lambda i: (1, 0)), VM, VM, VM],
        scratch_shapes=[
            pltpu.VMEM((PAIRS, PAIR, L), BF16),
            pltpu.VMEM((PAIRS, L, PAIR), BF16),
            pltpu.VMEM((PAIRS, PAIR, PREFIX), BF16),
            pltpu.VMEM((PAIRS, PREFIX, PAIR), BF16),
            pltpu.VMEM((PAIRS, L, PAIR), BF16),
            pltpu.VMEM((512, D), BF16),
            pltpu.VMEM((PAIRS, L, PAIR), F32),
        ],
        compiler_params=pltpu.CompilerParams(vmem_limit_bytes=VMEM_LIMIT),
        cost_estimate=pl.CostEstimate(flops=20_000_000_000, bytes_accessed=8_000_000, transcendentals=0),
        name="main_part",
    )(place, low, high, pre, table, w, w_out, *buckets)


def edge_kernel(
    place_ref, edge_ref, w_ref, w_out_ref, acc_ref, query_ref, gate_ref, prev_ref,
    out_hbm, keys, values, out_ref, sem,
):
    start = place_ref[0] * L
    length = place_ref[1]
    for t in range(2):
        at = slice(t * TILE, (t + 1) * TILE)
        rows = edge_ref[at, :]
        store_pairs(values, at, half_silu_proj(rows, w_ref[:, D : 2 * D]))
        store_turned(keys, at, half_silu_proj(rows, w_ref[:, 3 * D :]))
    first_head = head_masks()
    row = lax.broadcasted_iota(jnp.int32, (2 * TILE, TILE), 0)
    a = jnp.where(row < TILE, row, row - TILE)
    later = lax.broadcasted_iota(jnp.int32, (2 * TILE, TILE), 1) > a
    copies = []
    for t in range(2):
        here = slice(t * TILE, (t + 1) * TILE)
        columns = []
        for p in range(PAIRS):
            q = query_ref[p, here, :]
            zero = jnp.zeros_like(q)
            qq = jnp.concatenate([jnp.where(first_head, q, zero), jnp.where(first_head, zero, q)], axis=0)
            total = jnp.zeros((2 * TILE, PAIR), F32)
            for kt in range(t, 2):
                at = slice(kt * TILE, (kt + 1) * TILE)
                s = dot(qq, keys[p, :, at], ((1,), (0,)))
                if kt == t:
                    s = jnp.where(later, s, 0.0)
                w = silu_of_half(s).astype(BF16)
                total = total + dot(w, values[p, at, :], ((1,), (0,)))
            columns.append(acc_ref[p, here, :] + jnp.where(first_head, total[:TILE], total[TILE:]))
        whole = jnp.concatenate(columns, axis=1)
        out_ref[here, :] = finish(
            whole, gate_ref[here, :], row_scale(start + t * TILE, length), w_out_ref[...]
        )
        copies.append(pltpu.make_async_copy(out_ref.at[here], out_hbm.at[here], sem.at[t]))
        copies[t].start()
    for copy in copies:
        copy.wait()


def edge_part(place, edge, w, w_out, acc, query, gate, prev):
    return pl.pallas_call(
        edge_kernel,
        out_shape=jax.ShapeDtypeStruct((L, D), BF16),
        in_specs=[pl.BlockSpec(memory_space=pltpu.SMEM)] + [VM] * 6 + [pl.BlockSpec(memory_space=pl.ANY)],
        out_specs=pl.BlockSpec(memory_space=pl.ANY),
        input_output_aliases={7: 0},
        scratch_shapes=[
            pltpu.VMEM((PAIRS, PAIR, BAND), BF16),
            pltpu.VMEM((PAIRS, BAND, PAIR), BF16),
            pltpu.VMEM((2 * TILE, D), BF16),
            pltpu.SemaphoreType.DMA((2,)),
        ],
        compiler_params=pltpu.CompilerParams(vmem_limit_bytes=VMEM_LIMIT),
        name="edge_part",
    )(place, edge, w, w_out, acc, query, gate, prev)


def local(event_embed, event_time_bucket, time_table, history_length, w_proj, w_out):
    ctx = lax.axis_size("ctx")
    c = lax.axis_index("ctx").astype(jnp.int32)
    place = jnp.stack([c, history_length[0]])
    first = event_time_bucket[:, :PREFIX]
    buckets = [jnp.where(c == 0, first, 0)] + [lax.ppermute(first, "ctx", [(0, k)]) for k in range(1, ctx)]
    got = lax.all_to_all(pack(event_embed, ctx), ("users", "ctx"), split_axis=0, concat_axis=0, tiled=True)
    low, high, pre = norm(got, event_time_bucket, time_table)
    edge = lax.ppermute(high, "ctx", [(i, i + 1) for i in range(ctx - 1)])
    out, acc, query, gate = main_part(place, low, high, pre, time_table, w_proj, w_out, buckets)
    out = edge_part(place, edge, w_proj, w_out, acc, query, gate, out)
    return out[None]


def solution(mesh):
    return jax.shard_map(
        local,
        mesh=mesh,
        in_specs=(P(("users", "ctx"), None, None), P("users", "ctx"), P(), P("users"), P(), P()),
        out_specs=P("users", "ctx", None),
        check_vma=False,
    )
```
